32 devices in a mesh: rep: 8 (over y, x, core), hid: 4 (over z).
Axes of the slice: x: 2, y: 2, z: 4, core: 2. Of those that a mesh axis runs over, the one named last changes fastest.
Arguments:
- tokens: bfloat16 [2, 1024, 1152], P(None, ('rep', 'hid')), may hold values from -6 to 6
- targets: bfloat16 [2, 1024, 1152], P(None, ('rep', 'hid')), may hold values from -6 to 6
- w_gate: float32 [8, 6912, 1152], P('rep', 'hid'), may hold values from -6 to 6
- w_up: float32 [8, 6912, 1152], P('rep', 'hid'), may hold values from -6 to 6
- w_down: float32 [8, 6912, 1152], P('rep', 'hid'), may hold values from -6 to 6
Outputs:
- new_gate: float32 [8, 6912, 1152], P('rep', 'hid')
- new_up: float32 [8, 6912, 1152], P('rep', 'hid')
- new_down: float32 [8, 6912, 1152], P('rep', 'hid')
The draws below stay inside these ranges and needn't reach their ends.
All inputs are finite; a program needn't handle non-finite values.
Results may differ from the reference program's by a relative error of at most 0.0086.
Values may be sent and summed in bfloat16 or wider, within the bound.
A program may use at most 128 MiB of HBM per device.

```python
import jax
import jax.numpy as jnp
from jax import lax

D = 1152
FF = 6912
TOK_DEV = 32
STEPS = 2
TOKENS = 1024
REPLICAS = 8
N_REP = 8
N_HID = 4


def levels(rng, extent, shards, least, top_value):
    def one(position, parts):
        draws = jax.random.uniform(jax.random.fold_in(jax.random.fold_in(rng, 6), position), (parts,), jnp.float32, least / len(shards), top_value / len(shards))
        return jnp.repeat(jnp.exp(draws), extent[position] // parts).reshape((-1,) + (1,) * (len(extent) - position - 1))

    loudness = one(*shards[0])
    for cut in shards[1:]:
        loudness = loudness * one(*cut)
    return loudness


def scatter_about(key, shape, width, most, pieces=(), kind=jnp.bfloat16):
    entries = jax.random.normal(key, shape, jnp.float32) * width
    if len(pieces) > 0:
        entries = levels(key, shape, pieces, -0.22, 0.18) * entries
    return jnp.clip(entries, min=-most, max=most).astype(kind)


def setup_inputs(seed: int = 0) -> dict:
    streams_of = jax.random.split(jax.random.key(seed), 6)
    return {
        "tokens": scatter_about(streams_of[0], (STEPS, TOKENS, D), 1.0, 6.0, ((1, 32),)),
        "targets": scatter_about(streams_of[1], (STEPS, TOKENS, D), 1.0, 6.0, ((1, 32),)),
        "w_gate": scatter_about(streams_of[2], (REPLICAS, FF, D), 1.0, 6.0, ((0, 8), (1, 4)), jnp.float32),
        "w_up": scatter_about(streams_of[3], (REPLICAS, FF, D), 1.0, 6.0, ((0, 8), (1, 4)), jnp.float32),
        "w_down": scatter_about(streams_of[4], (REPLICAS, FF, D), 1.0, 6.0, ((0, 8), (1, 4)), jnp.float32),
    }


LEARNING_RATE = 0.5

def gelu_tanh(value):
    return jax.nn.gelu(value, approximate=True)

def contract_cols(left, right):
    return lax.dot_general(left, right, (((1,), (1,)), ((), ())), preferred_element_type=jnp.float32)

def contract_rows(left, right):
    return lax.dot_general(left, right, (((0,), (0,)), ((), ())), preferred_element_type=jnp.float32)

def replica_update(packed):
    gate_weight, up_weight, down_weight, token_batch, target_rows = packed
    scale_model = float(D) ** (-0.5)
    scale_hidden = float(FF) ** (-0.5)
    gate_half = gate_weight.astype(jnp.bfloat16)
    up_half = up_weight.astype(jnp.bfloat16)
    down_half = down_weight.astype(jnp.bfloat16)
    gate_value = contract_cols(token_batch, gate_half) * scale_model
    up_value = contract_cols(token_batch, up_half) * scale_model
    activated, gelu_back = jax.vjp(gelu_tanh, gate_value)
    hidden = (activated * up_value).astype(jnp.bfloat16)
    output = jnp.dot(hidden, down_half, preferred_element_type=jnp.float32) * scale_hidden
    residual = (output - target_rows.astype(jnp.float32)).astype(jnp.bfloat16)
    grad_down = contract_rows(hidden, residual) * scale_hidden
    hidden_grad = contract_cols(residual, down_half) * scale_hidden
    gate_grad = gelu_back(hidden_grad * up_value)[0].astype(jnp.bfloat16)
    up_grad = (hidden_grad * activated).astype(jnp.bfloat16)
    grad_gate = contract_rows(gate_grad, token_batch) * scale_model
    grad_up = contract_rows(up_grad, token_batch) * scale_model
    return (gate_weight - LEARNING_RATE * grad_gate, up_weight - LEARNING_RATE * grad_up, down_weight - LEARNING_RATE * grad_down)

def average_pairs(weight, stride):
    grouped = weight.reshape(N_REP // (2 * stride), 2, stride, FF, D)
    averaged = (grouped[:, 0] + grouped[:, 1]) * 0.5
    return jnp.stack([averaged, averaged], axis=1).reshape(N_REP, FF, D)

def reference(tokens, targets, w_gate, w_up, w_down):
    weights = (w_gate, w_up, w_down)
    for step_index in range(STEPS):
        token_batch = tokens[step_index].reshape(N_REP, TOK_DEV * N_HID, D)
        target_rows = targets[step_index].reshape(N_REP, TOK_DEV * N_HID, D)
        stepped = lax.map(replica_update, weights + (token_batch, target_rows))
        weights = tuple((average_pairs(weight, 2 ** step_index) for weight in stepped))
    return (weights[0], weights[1], weights[2])
```

```python
import jax
import jax.numpy as jnp
from jax import lax
from jax.sharding import PartitionSpec as P

LEARNING_RATE = 0.5
LINK_SCALE = 8192.0


def swapped(value, axis, distance):
    pairs = [(source, source ^ distance) for source in range(lax.axis_size(axis))]
    return lax.ppermute(value, axis, pairs)


def gelu_tanh(value):
    return jax.nn.gelu(value, approximate=True)


def contract_cols(left, right):
    return lax.dot_general(
        left, right, (((1,), (1,)), ((), ())), preferred_element_type=jnp.float32
    )


def contract_rows(left, right):
    return lax.dot_general(
        left, right, (((0,), (0,)), ((), ())), preferred_element_type=jnp.float32
    )


def to_link(value):
    return (value * LINK_SCALE).astype(jnp.float16)


def from_link(value):
    return value.astype(jnp.float32) * (1.0 / LINK_SCALE)


def factors(tokens, targets, weights, scale_model, scale_hidden):
    gate_half, up_half, down_half = weights
    gate_value = contract_cols(tokens, gate_half) * scale_model
    up_value = contract_cols(tokens, up_half) * scale_model
    activated, gelu_back = jax.vjp(gelu_tanh, gate_value)
    hidden = (activated * up_value).astype(jnp.bfloat16)
    partial_out = (
        jnp.dot(hidden, down_half, preferred_element_type=jnp.float32) * scale_hidden
    )
    output = lax.psum(partial_out, "hid")
    residual = (output - targets.astype(jnp.float32)).astype(jnp.bfloat16)
    hidden_grad = contract_cols(residual, down_half) * scale_hidden
    gate_grad = gelu_back(hidden_grad * up_value)[0].astype(jnp.bfloat16)
    up_grad = (hidden_grad * activated).astype(jnp.bfloat16)
    return gate_grad, up_grad, hidden, residual


def local(tokens, targets, w_gate, w_up, w_down):
    hid = lax.axis_size("hid")
    features = w_gate.shape[2]
    rows = w_gate.shape[1]
    scale_model = float(features) ** (-0.5)
    scale_hidden = float(rows * hid) ** (-0.5)
    scales = (scale_model, scale_model, scale_hidden)
    core = lax.rem(lax.axis_index("rep"), 2)
    weights = (w_gate[0], w_up[0], w_down[0])
    half = rows // 2

    all_tokens = lax.all_gather(tokens, "hid", axis=1, tiled=True)
    all_targets = lax.all_gather(targets, "hid", axis=1, tiled=True)

    means = []
    for weight in weights:
        theirs = swapped(to_link(weight), "rep", 1)
        means.append((weight + from_link(theirs)) * 0.5)
    far = []
    for mean in means:
        part = lax.dynamic_slice_in_dim(mean, core * half, half, 0)
        far.append(swapped(to_link(part), "rep", 2))
    near = [swapped(part, "rep", 1) for part in far]

    own = factors(
        all_tokens[0],
        all_targets[0],
        tuple(w.astype(jnp.bfloat16) for w in weights),
        scale_model,
        scale_hidden,
    )
    own = (*own, all_tokens[0])
    pair = swapped(own, "rep", 1)
    far_zero = swapped(own, "rep", 2)
    near_zero = swapped(far_zero, "rep", 1)
    stepped = []
    for index in range(3):
        right = 3 if index == 2 else 4
        grad = contract_rows(
            jnp.concatenate([own[index], pair[index]]),
            jnp.concatenate([own[right], pair[right]]),
        )
        stepped.append(
            means[index] - grad * (0.5 * LEARNING_RATE * scales[index])
        )

    mine = factors(
        all_tokens[1],
        all_targets[1],
        tuple(w.astype(jnp.bfloat16) for w in stepped),
        scale_model,
        scale_hidden,
    )
    mine = (*mine, all_tokens[1])
    far_one = swapped(mine, "rep", 2)
    out = []
    for index in range(3):
        right = 3 if index == 2 else 4
        grad = contract_rows(
            jnp.concatenate(
                [far_zero[index], near_zero[index], mine[index] * 2, far_one[index] * 2]
            ),
            jnp.concatenate(
                [far_zero[right], near_zero[right], mine[right], far_one[right]]
            ),
        )
        low = jnp.where(core == 0, far[index], near[index])
        high = jnp.where(core == 0, near[index], far[index])
        other = from_link(jnp.concatenate([low, high]))
        out.append(
            ((stepped[index] + other) * 0.5
             - grad * (0.25 * LEARNING_RATE * scales[index]))[None]
        )
    return tuple(out)


def solution(mesh):
    rows = P(None, ("rep", "hid"), None)
    weight = P("rep", "hid", None)
    return jax.shard_map(
        local,
        mesh=mesh,
        in_specs=(rows, rows, weight, weight, weight),
        out_specs=(weight, weight, weight),
        check_vma=False,
    )
```

```python
import jax
import jax.numpy as jnp
from jax import lax
from jax.sharding import PartitionSpec as P

LEARNING_RATE = 0.5
LINK_SCALE = 8192.0


def swapped(value, axis, distance):
    pairs = [(source, source ^ distance) for source in range(lax.axis_size(axis))]
    return lax.ppermute(value, axis, pairs)


def gathered(value, axis, dim):
    size = lax.axis_size(axis)
    me = lax.axis_index(axis)
    shards = [value]
    for shift in range(1, size):
        pairs = [(source, (source - shift) % size) for source in range(size)]
        shards.append(lax.ppermute(value, axis, pairs))
    twice = jnp.concatenate(shards + shards[:-1], axis=dim)
    width = value.shape[dim]
    start = lax.rem(size - me, size) * width
    return lax.dynamic_slice_in_dim(twice, start, size * width, dim)


def gelu_tanh(value):
    return jax.nn.gelu(value, approximate=True)


def contract_cols(left, right):
    return lax.dot_general(
        left, right, (((1,), (1,)), ((), ())), preferred_element_type=jnp.float32
    )


def contract_rows(left, right):
    return lax.dot_general(
        left, right, (((0,), (0,)), ((), ())), preferred_element_type=jnp.float32
    )


def to_link(value):
    return (value * LINK_SCALE).astype(jnp.float16)


def from_link(value):
    return value.astype(jnp.float32) * (1.0 / LINK_SCALE)


def in_order(core, own, other):
    low = jnp.where(core == 0, own, other)
    high = jnp.where(core == 0, other, own)
    return jnp.concatenate([low, high])


def factors(tokens, targets, weights, scale_model, scale_hidden):
    gate_half, up_half, down_half = weights
    gate_value = contract_cols(tokens, gate_half) * scale_model
    up_value = contract_cols(tokens, up_half) * scale_model
    activated, gelu_back = jax.vjp(gelu_tanh, gate_value)
    hidden = (activated * up_value).astype(jnp.bfloat16)
    partial_out = (
        jnp.dot(hidden, down_half, preferred_element_type=jnp.float32) * scale_hidden
    )
    output = lax.psum(partial_out, "hid")
    residual = (output - targets.astype(jnp.float32)).astype(jnp.bfloat16)
    hidden_grad = contract_cols(residual, down_half) * scale_hidden
    gate_grad = gelu_back(hidden_grad * up_value)[0].astype(jnp.bfloat16)
    up_grad = (hidden_grad * activated).astype(jnp.bfloat16)
    return jnp.concatenate([gate_grad, up_grad, hidden], axis=1), residual


def gradients(lefts, residuals, tokens):
    left = jnp.concatenate(lefts)
    rows = left.shape[1] // 3
    right = (jnp.concatenate(tokens),) * 2 + (jnp.concatenate(residuals),)
    return [
        contract_rows(left[:, index * rows : (index + 1) * rows], right[index])
        for index in range(3)
    ]


def local(tokens, targets, w_gate, w_up, w_down):
    hid = lax.axis_size("hid")
    features = w_gate.shape[2]
    rows = w_gate.shape[1]
    scale_model = float(features) ** (-0.5)
    scale_hidden = float(rows * hid) ** (-0.5)
    scales = (scale_model, scale_model, scale_hidden)
    core = lax.rem(lax.axis_index("rep"), 2)
    weights = (w_gate[0], w_up[0], w_down[0])
    half = rows // 2

    given = [
        to_link(lax.dynamic_slice_in_dim(w, (1 - core) * half, half, 0))
        for w in weights
    ]
    given, tokens, targets = lax.optimization_barrier((given, tokens, targets))
    taken = [swapped(part, "rep", 1) for part in given]
    both = gathered(jnp.concatenate([tokens, targets]), "hid", 1)
    means = [
        to_link(
            (lax.dynamic_slice_in_dim(w, core * half, half, 0) + from_link(part)) * 0.5
        )
        for w, part in zip(weights, taken)
    ]
    means, both = lax.optimization_barrier((means, both))
    far = [swapped(part, "rep", 2) for part in means]
    pair_means = [swapped(part, "rep", 1) for part in means]
    all_tokens, all_targets = both[:2], both[2:]
    pair_tokens = swapped(all_tokens, "rep", 1)
    far_tokens = gathered(swapped(tokens, "rep", 2), "hid", 1)
    near_tokens = swapped(far_tokens[0], "rep", 1)

    left, residual = factors(
        all_tokens[0],
        all_targets[0],
        tuple(w.astype(jnp.bfloat16) for w in weights),
        scale_model,
        scale_hidden,
    )
    pair_left, pair_residual = swapped((left, residual), "rep", 1)
    far_left, far_residual = swapped((left, residual), "rep", 2)
    near_left, near_residual = swapped((far_left, far_residual), "rep", 1)
    grads = gradients(
        (left, pair_left), (residual, pair_residual), (all_tokens[0], pair_tokens[0])
    )
    stepped = [
        from_link(in_order(core, mean, other)) - grad * (0.5 * LEARNING_RATE * scale)
        for mean, other, grad, scale in zip(means, pair_means, grads, scales)
    ]

    mine, my_residual = factors(
        all_tokens[1],
        all_targets[1],
        tuple(w.astype(jnp.bfloat16) for w in stepped),
        scale_model,
        scale_hidden,
    )
    theirs, their_residual = swapped((mine, my_residual), "rep", 2)
    near = [swapped(part, "rep", 1) for part in far]
    grads = gradients(
        (far_left, near_left), (far_residual, near_residual), (far_tokens[0], near_tokens)
    )
    base = [
        (weight + from_link(in_order(core, own, other))) * 0.5
        - grad * (0.25 * LEARNING_RATE * scale)
        for weight, own, other, grad, scale in zip(stepped, far, near, grads, scales)
    ]
    base = lax.optimization_barrier(base)
    grads = gradients(
        (mine, theirs), (my_residual, their_residual), (all_tokens[1], far_tokens[1])
    )
    return tuple(
        (weight - grad * (0.5 * LEARNING_RATE * scale))[None]
        for weight, grad, scale in zip(base, grads, scales)
    )


def solution(mesh):
    rows = P(None, ("rep", "hid"), None)
    weight = P("rep", "hid", None)
    return jax.shard_map(
        local,
        mesh=mesh,
        in_specs=(rows, rows, weight, weight, weight),
        out_specs=(weight, weight, weight),
        check_vma=False,
    )
```

```python
import jax
import jax.numpy as jnp
from jax import lax
from jax.sharding import PartitionSpec as P

LEARNING_RATE = 0.5
LINK_SCALE = 8192.0


def swapped(value, axis, distance):
    pairs = [(source, source ^ distance) for source in range(lax.axis_size(axis))]
    return lax.ppermute(value, axis, pairs)


def gathered(value, axis, dim):
    size = lax.axis_size(axis)
    me = lax.axis_index(axis)
    width = value.shape[dim]
    whole = jnp.zeros(
        value.shape[:dim] + (size * width,) + value.shape[dim + 1 :], value.dtype
    )
    for shift in range(size):
        shard = value
        if shift > 0:
            pairs = [(source, (source - shift) % size) for source in range(size)]
            shard = lax.ppermute(value, axis, pairs)
        owner = lax.rem(me + shift, size)
        whole = lax.dynamic_update_slice_in_dim(whole, shard, owner * width, dim)
    return whole


def scattered_sum(value, axis):
    size = lax.axis_size(axis)
    me = lax.axis_index(axis)
    width = value.shape[0] // size
    total = lax.dynamic_slice_in_dim(value, me * width, width, 0)
    for shift in range(1, size):
        pairs = [(source, (source + shift) % size) for source in range(size)]
        target = lax.rem(me + shift, size)
        chunk = lax.dynamic_slice_in_dim(value, target * width, width, 0)
        total = total + lax.ppermute(chunk, axis, pairs)
    return total


def gelu_tanh(value):
    return jax.nn.gelu(value, approximate=True)


def contract_cols(left, right):
    return lax.dot_general(
        left, right, (((1,), (1,)), ((), ())), preferred_element_type=jnp.float32
    )


def contract_rows(left, right):
    return lax.dot_general(
        left, right, (((0,), (0,)), ((), ())), preferred_element_type=jnp.float32
    )


def to_link(value):
    return (value * LINK_SCALE).astype(jnp.float16)


def from_link(value):
    return value.astype(jnp.float32) * (1.0 / LINK_SCALE)


def in_order(core, own, other):
    low = jnp.where(core == 0, own, other)
    high = jnp.where(core == 0, other, own)
    return jnp.concatenate([low, high])


def factors(tokens, targets, weights, arrivals, scale_model, scale_hidden):
    gate_half, up_half, down_half = weights
    gate_value = contract_cols(tokens, gate_half) * scale_model
    up_value = contract_cols(tokens, up_half) * scale_model
    activated, gelu_back = jax.vjp(gelu_tanh, gate_value)
    hidden = (activated * up_value).astype(jnp.bfloat16)
    partial_out = (
        jnp.dot(hidden, down_half, preferred_element_type=jnp.float32) * scale_hidden
    )
    output = scattered_sum(partial_out, "hid")
    residual = (output - targets.astype(jnp.float32)).astype(jnp.bfloat16)
    residual, arrivals = lax.optimization_barrier((residual, arrivals))
    residual = gathered(residual, "hid", 0)
    hidden_grad = contract_cols(residual, down_half) * scale_hidden
    gate_grad = gelu_back(hidden_grad * up_value)[0].astype(jnp.bfloat16)
    up_grad = (hidden_grad * activated).astype(jnp.bfloat16)
    left = jnp.concatenate([gate_grad, up_grad, hidden], axis=1)
    return left, residual, arrivals


def gradients(lefts, residuals, tokens):
    left = jnp.concatenate(lefts)
    rows = left.shape[1] // 3
    right = (jnp.concatenate(tokens),) * 2 + (jnp.concatenate(residuals),)
    return [
        contract_rows(left[:, index * rows : (index + 1) * rows], right[index])
        for index in range(3)
    ]


def local(tokens, targets, w_gate, w_up, w_down):
    hid = lax.axis_size("hid")
    features = w_gate.shape[2]
    rows = w_gate.shape[1]
    scale_model = float(features) ** (-0.5)
    scale_hidden = float(rows * hid) ** (-0.5)
    scales = (scale_model, scale_model, scale_hidden)
    core = lax.rem(lax.axis_index("rep"), 2)
    weights = (w_gate[0], w_up[0], w_down[0])
    half = rows // 2

    given = [
        to_link(lax.dynamic_slice_in_dim(w, (1 - core) * half, half, 0))
        for w in weights
    ]
    given, tokens, targets = lax.optimization_barrier((given, tokens, targets))
    taken = [swapped(part, "rep", 1) for part in given]
    all_tokens = gathered(tokens, "hid", 1)
    means = [
        to_link(
            (lax.dynamic_slice_in_dim(w, core * half, half, 0) + from_link(part)) * 0.5
        )
        for w, part in zip(weights, taken)
    ]
    means, all_tokens = lax.optimization_barrier((means, all_tokens))
    far = [swapped(part, "rep", 2) for part in means]
    pair_means = [swapped(part, "rep", 1) for part in means]
    pair_tokens = swapped(all_tokens, "rep", 1)
    far_tokens = gathered(swapped(tokens, "rep", 2), "hid", 1)
    near_tokens = swapped(far_tokens[0], "rep", 1)

    left, residual, far[:2] = factors(
        all_tokens[0],
        targets[0],
        tuple(w.astype(jnp.bfloat16) for w in weights),
        far[:2],
        scale_model,
        scale_hidden,
    )
    pair_left, pair_residual = swapped((left, residual), "rep", 1)
    far_left, far_residual = swapped((left, residual), "rep", 2)
    grads = gradients(
        (left, pair_left), (residual, pair_residual), (all_tokens[0], pair_tokens[0])
    )
    stepped = [
        from_link(in_order(core, mean, other)) - grad * (0.5 * LEARNING_RATE * scale)
        for mean, other, grad, scale in zip(means, pair_means, grads, scales)
    ]

    stepped, far[2] = lax.optimization_barrier((stepped, far[2]))

    mine, my_residual, (far_left, far_residual) = factors(
        all_tokens[1],
        targets[1],
        tuple(w.astype(jnp.bfloat16) for w in stepped),
        (far_left, far_residual),
        scale_model,
        scale_hidden,
    )
    theirs, their_residual = swapped((mine, my_residual), "rep", 2)
    near_left, near_residual = swapped((far_left, far_residual), "rep", 1)
    near = [swapped(part, "rep", 1) for part in far]
    grads = gradients(
        (far_left, near_left), (far_residual, near_residual), (far_tokens[0], near_tokens)
    )
    base = [
        (weight + from_link(in_order(core, own, other))) * 0.5
        - grad * (0.25 * LEARNING_RATE * scale)
        for weight, own, other, grad, scale in zip(stepped, far, near, grads, scales)
    ]
    base = lax.optimization_barrier(base)
    grads = gradients(
        (mine, theirs), (my_residual, their_residual), (all_tokens[1], far_tokens[1])
    )
    return tuple(
        (weight - grad * (0.5 * LEARNING_RATE * scale))[None]
        for weight, grad, scale in zip(base, grads, scales)
    )


def solution(mesh):
    rows = P(None, ("rep", "hid"), None)
    weight = P("rep", "hid", None)
    return jax.shard_map(
        local,
        mesh=mesh,
        in_specs=(rows, rows, weight, weight, weight),
        out_specs=(weight, weight, weight),
        check_vma=False,
    )
```

```python
import jax
import jax.numpy as jnp
from jax import lax
from jax.sharding import PartitionSpec as P

LEARNING_RATE = 0.5
LINK_SCALE = 8192.0


def swapped(value, axis, distance):
    pairs = [(source, source ^ distance) for source in range(lax.axis_size(axis))]
    return lax.ppermute(value, axis, pairs)


def gathered(value, axis, dim):
    size = lax.axis_size(axis)
    me = lax.axis_index(axis)
    width = value.shape[dim]
    whole = jnp.zeros(
        value.shape[:dim] + (size * width,) + value.shape[dim + 1 :], value.dtype
    )
    for shift in range(size):
        shard = value
        if shift > 0:
            pairs = [(source, (source - shift) % size) for source in range(size)]
            shard = lax.ppermute(value, axis, pairs)
        owner = lax.rem(me + shift, size)
        whole = lax.dynamic_update_slice_in_dim(whole, shard, owner * width, dim)
    return whole


def scattered_sum(value, axis):
    size = lax.axis_size(axis)
    me = lax.axis_index(axis)
    width = value.shape[0] // size
    total = lax.dynamic_slice_in_dim(value, me * width, width, 0)
    for shift in range(1, size):
        pairs = [(source, (source + shift) % size) for source in range(size)]
        target = lax.rem(me + shift, size)
        chunk = lax.dynamic_slice_in_dim(value, target * width, width, 0)
        total = total + lax.ppermute(chunk, axis, pairs)
    return total


def gelu_tanh(value):
    return jax.nn.gelu(value, approximate=True)


def contract_cols(left, right):
    return lax.dot_general(
        left, right, (((1,), (1,)), ((), ())), preferred_element_type=jnp.float32
    )


def contract_rows(left, right):
    return lax.dot_general(
        left, right, (((0,), (0,)), ((), ())), preferred_element_type=jnp.float32
    )


def to_link(value):
    return (value * LINK_SCALE).astype(jnp.float16)


def from_link(value):
    return value.astype(jnp.float32) * (1.0 / LINK_SCALE)


def in_order(core, own, other):
    low = jnp.where(core == 0, own, other)
    high = jnp.where(core == 0, other, own)
    return jnp.concatenate([low, high])


def factors(tokens, targets, weights, arrivals, scale_model, scale_hidden):
    gate_half, up_half, down_half = weights
    gate_value = contract_cols(tokens, gate_half) * scale_model
    up_value = contract_cols(tokens, up_half) * scale_model
    activated, gelu_back = jax.vjp(gelu_tanh, gate_value)
    hidden = (activated * up_value).astype(jnp.bfloat16)
    partial_out = (
        jnp.dot(hidden, down_half, preferred_element_type=jnp.float32) * scale_hidden
    )
    output = scattered_sum(partial_out, "hid")
    residual = (output - targets.astype(jnp.float32)).astype(jnp.bfloat16)
    residual, arrivals = lax.optimization_barrier((residual, arrivals))
    residual = gathered(residual, "hid", 0)
    hidden_grad = contract_cols(residual, down_half) * scale_hidden
    gate_grad = gelu_back(hidden_grad * up_value)[0].astype(jnp.bfloat16)
    up_grad = (hidden_grad * activated).astype(jnp.bfloat16)
    left = jnp.concatenate([gate_grad, up_grad, hidden], axis=1)
    return left, residual, arrivals


def gradients(lefts, residuals, tokens):
    left = jnp.concatenate(lefts)
    rows = left.shape[1] // 3
    right = (jnp.concatenate(tokens),) * 2 + (jnp.concatenate(residuals),)
    return [
        contract_rows(left[:, index * rows : (index + 1) * rows], right[index])
        for index in range(3)
    ]


def local(tokens, targets, w_gate, w_up, w_down):
    hid = lax.axis_size("hid")
    features = w_gate.shape[2]
    rows = w_gate.shape[1]
    scale_model = float(features) ** (-0.5)
    scale_hidden = float(rows * hid) ** (-0.5)
    scales = (scale_model, scale_model, scale_hidden)
    core = lax.rem(lax.axis_index("rep"), 2)
    weights = (w_gate[0], w_up[0], w_down[0])
    half = rows // 2

    given = [
        to_link(lax.dynamic_slice_in_dim(w, (1 - core) * half, half, 0))
        for w in weights
    ]
    taken = [swapped(part, "rep", 1) for part in given]
    far_shard = swapped(tokens, "rep", 2)
    taken, tokens, far_shard = lax.optimization_barrier((taken, tokens, far_shard))
    all_tokens = gathered(tokens, "hid", 1)
    means = [
        to_link(
            (lax.dynamic_slice_in_dim(w, core * half, half, 0) + from_link(part)) * 0.5
        )
        for w, part in zip(weights, taken)
    ]
    means, all_tokens = lax.optimization_barrier((means, all_tokens))
    far = [swapped(part, "rep", 2) for part in means]
    pair_means = [swapped(part, "rep", 1) for part in means]
    pair_tokens = swapped(all_tokens[0], "rep", 1)

    left, residual, far[0] = factors(
        all_tokens[0],
        targets[0],
        tuple(w.astype(jnp.bfloat16) for w in weights),
        far[0],
        scale_model,
        scale_hidden,
    )
    left, far[1], far_shard = lax.optimization_barrier((left, far[1], far_shard))
    pair_left, pair_residual = swapped((left, residual), "rep", 1)
    far_left, far_residual = swapped((left, residual), "rep", 2)
    grads = gradients(
        (left, pair_left), (residual, pair_residual), (all_tokens[0], pair_tokens)
    )
    stepped = [
        from_link(in_order(core, mean, other)) - grad * (0.5 * LEARNING_RATE * scale)
        for mean, other, grad, scale in zip(means, pair_means, grads, scales)
    ]

    far_tokens = gathered(far_shard, "hid", 1)
    near_tokens = swapped(far_tokens[0], "rep", 1)

    mine, my_residual, (far_left, far_residual) = factors(
        all_tokens[1],
        targets[1],
        tuple(w.astype(jnp.bfloat16) for w in stepped),
        (far_left, far_residual),
        scale_model,
        scale_hidden,
    )
    theirs, their_residual = swapped((mine, my_residual), "rep", 2)
    near_left, near_residual = swapped((far_left, far_residual), "rep", 1)
    near = [swapped(part, "rep", 1) for part in far]
    grads = gradients(
        (far_left, near_left, mine * 2),
        (far_residual, near_residual, my_residual),
        (far_tokens[0], near_tokens, all_tokens[1]),
    )
    base = [
        (weight + from_link(in_order(core, own, other))) * 0.5
        - grad * (0.25 * LEARNING_RATE * scale)
        for weight, own, other, grad, scale in zip(stepped, far, near, grads, scales)
    ]
    base, theirs, their_residual = lax.optimization_barrier(
        (base, theirs, their_residual)
    )
    grads = gradients((theirs,), (their_residual,), (far_tokens[1],))
    return tuple(
        (weight - grad * (0.5 * LEARNING_RATE * scale))[None]
        for weight, grad, scale in zip(base, grads, scales)
    )


def solution(mesh):
    rows = P(None, ("rep", "hid"), None)
    weight = P("rep", "hid", None)
    return jax.shard_map(
        local,
        mesh=mesh,
        in_specs=(rows, rows, weight, weight, weight),
        out_specs=(weight, weight, weight),
        check_vma=False,
    )
```

```python
import jax
import jax.numpy as jnp
from jax import lax
from jax.sharding import PartitionSpec as P

LEARNING_RATE = 0.5
LINK_SCALE = 8192.0


def swapped(value, axis, distance):
    pairs = [(source, source ^ distance) for source in range(lax.axis_size(axis))]
    return lax.ppermute(value, axis, pairs)


def gathered(value, axis, dim):
    size = lax.axis_size(axis)
    me = lax.axis_index(axis)
    width = value.shape[dim]
    whole = jnp.zeros(
        value.shape[:dim] + (size * width,) + value.shape[dim + 1 :], value.dtype
    )
    for shift in range(size):
        shard = value
        if shift > 0:
            pairs = [(source, (source - shift) % size) for source in range(size)]
            shard = lax.ppermute(value, axis, pairs)
        owner = lax.rem(me + shift, size)
        whole = lax.dynamic_update_slice_in_dim(whole, shard, owner * width, dim)
    return whole


def scattered_sum(value, axis):
    size = lax.axis_size(axis)
    me = lax.axis_index(axis)
    width = value.shape[0] // size
    total = lax.dynamic_slice_in_dim(value, me * width, width, 0)
    for shift in range(1, size):
        pairs = [(source, (source + shift) % size) for source in range(size)]
        target = lax.rem(me + shift, size)
        chunk = lax.dynamic_slice_in_dim(value, target * width, width, 0)
        total = total + lax.ppermute(chunk, axis, pairs)
    return total


def gelu_tanh(value):
    return jax.nn.gelu(value, approximate=True)


def contract_cols(left, right):
    return lax.dot_general(
        left, right, (((1,), (1,)), ((), ())), preferred_element_type=jnp.float32
    )


def contract_rows(left, right):
    return lax.dot_general(
        left, right, (((0,), (0,)), ((), ())), preferred_element_type=jnp.float32
    )


def to_link(value):
    return (value * LINK_SCALE).astype(jnp.float16)


def from_link(value):
    return value.astype(jnp.float32) * (1.0 / LINK_SCALE)


def in_order(core, own, other):
    low = jnp.where(core == 0, own, other)
    high = jnp.where(core == 0, other, own)
    return jnp.concatenate([low, high])


def factors(tokens, targets, weights, arrivals, scale_model, scale_hidden):
    gate_half, up_half, down_half = weights
    gate_value = contract_cols(tokens, gate_half) * scale_model
    up_value = contract_cols(tokens, up_half) * scale_model
    activated, gelu_back = jax.vjp(gelu_tanh, gate_value)
    hidden = (activated * up_value).astype(jnp.bfloat16)
    partial_out = (
        jnp.dot(hidden, down_half, preferred_element_type=jnp.float32) * scale_hidden
    )
    output = scattered_sum(partial_out, "hid")
    residual = (output - targets.astype(jnp.float32)).astype(jnp.bfloat16)
    residual, arrivals = lax.optimization_barrier((residual, arrivals))
    residual = gathered(residual, "hid", 0)
    hidden_grad = contract_cols(residual, down_half) * scale_hidden
    gate_grad = gelu_back(hidden_grad * up_value)[0].astype(jnp.bfloat16)
    up_grad = (hidden_grad * activated).astype(jnp.bfloat16)
    left = jnp.concatenate([gate_grad, up_grad, hidden], axis=1)
    return left, residual, arrivals


def gradients(lefts, residuals, tokens):
    left = jnp.concatenate(lefts)
    rows = left.shape[1] // 3
    right = (jnp.concatenate(tokens),) * 2 + (jnp.concatenate(residuals),)
    return [
        contract_rows(left[:, index * rows : (index + 1) * rows], right[index])
        for index in range(3)
    ]


def local(tokens, targets, w_gate, w_up, w_down):
    hid = lax.axis_size("hid")
    features = w_gate.shape[2]
    rows = w_gate.shape[1]
    scale_model = float(features) ** (-0.5)
    scale_hidden = float(rows * hid) ** (-0.5)
    scales = (scale_model, scale_model, scale_hidden)
    core = lax.rem(lax.axis_index("rep"), 2)
    weights = (w_gate[0], w_up[0], w_down[0])
    half = rows // 2

    given = [
        to_link(lax.dynamic_slice_in_dim(w, (1 - core) * half, half, 0))
        for w in weights
    ]
    taken = [swapped(part, "rep", 1) for part in given]
    far_shard = swapped(tokens, "rep", 2)
    taken, tokens, far_shard = lax.optimization_barrier((taken, tokens, far_shard))
    all_tokens = gathered(tokens, "hid", 1)
    means = [
        to_link(
            (lax.dynamic_slice_in_dim(w, core * half, half, 0) + from_link(part)) * 0.5
        )
        for w, part in zip(weights, taken)
    ]
    means, all_tokens = lax.optimization_barrier((means, all_tokens))
    far = [swapped(part, "rep", 2) for part in means]
    pair_means = [swapped(part, "rep", 1) for part in means]
    pair_tokens = swapped(all_tokens[0], "rep", 1)

    left, residual, far[0] = factors(
        all_tokens[0],
        targets[0],
        tuple(w.astype(jnp.bfloat16) for w in weights),
        far[0],
        scale_model,
        scale_hidden,
    )
    left, far[1], far_shard = lax.optimization_barrier((left, far[1], far_shard))
    pair_left, pair_residual = swapped((left, residual), "rep", 1)
    far_left, far_residual = swapped((left, residual), "rep", 2)
    grads = gradients(
        (left, pair_left), (residual, pair_residual), (all_tokens[0], pair_tokens)
    )
    stepped = [
        from_link(in_order(core, mean, other)) - grad * (0.5 * LEARNING_RATE * scale)
        for mean, other, grad, scale in zip(means, pair_means, grads, scales)
    ]

    far_tokens = gathered(far_shard, "hid", 1)
    near_tokens = swapped(far_tokens[0], "rep", 1)

    near = [swapped(part, "rep", 1) for part in far]
    others = [in_order(core, *parts) for parts in zip(far, near)]
    mine, my_residual, others = factors(
        all_tokens[1],
        targets[1],
        tuple(w.astype(jnp.bfloat16) for w in stepped),
        others,
        scale_model,
        scale_hidden,
    )
    mine, far_left, far_residual = lax.optimization_barrier(
        (mine, far_left, far_residual)
    )
    theirs, their_residual = swapped((mine, my_residual), "rep", 2)
    near_left, near_residual = swapped((far_left, far_residual), "rep", 1)
    grads = gradients(
        (far_left, near_left), (far_residual, near_residual), (far_tokens[0], near_tokens)
    )
    base = [
        (weight + from_link(other)) * 0.5 - grad * (0.25 * LEARNING_RATE * scale)
        for weight, other, grad, scale in zip(stepped, others, grads, scales)
    ]
    base = lax.optimization_barrier(base)
    grads = gradients(
        (mine, theirs), (my_residual, their_residual), (all_tokens[1], far_tokens[1])
    )
    return tuple(
        (weight - grad * (0.5 * LEARNING_RATE * scale))[None]
        for weight, grad, scale in zip(base, grads, scales)
    )


def solution(mesh):
    rows = P(None, ("rep", "hid"), None)
    weight = P("rep", "hid", None)
    return jax.shard_map(
        local,
        mesh=mesh,
        in_specs=(rows, rows, weight, weight, weight),
        out_specs=(weight, weight, weight),
        check_vma=False,
    )
```
